512 devices in a mesh: grp: 16 (over x, z_hi, core), hid: 32 (over y, z_lo).
Axes of the slice: x: 4, y: 4, z: 16 (z_hi: 2, z_lo: 8; z = z_hi * 8 + z_lo), core: 2. Of those that a mesh axis runs over, the one named last changes fastest.
Arguments:
- acts: bfloat16 [2, 512, 64, 4096], P(None, 'grp', None, 'hid'), may hold values from -6 to 6
- cotangents: bfloat16 [2, 512, 64, 4096], P(None, 'grp', None, 'hid'), may hold values from -6 to 6
- adapter_down_weight: bfloat16 [2, 16, 4096], P(None, None, 'hid'), may hold values from -0.09375 to 0.09375
- adapter_up_weight: bfloat16 [2, 4096, 16], P(None, 'hid'), may hold values from -0.09375 to 0.09375
- lengths: int32 [512], P('grp'), may hold values from 17 to 64
Outputs:
- similarity: float32 [512, 512], P('hid', 'grp')
The draws below stay inside these ranges and needn't reach their ends.
All inputs are finite; a program needn't handle non-finite values.
Results may differ from the reference program's by a relative error of at most 0.00089.
Values may be sent and summed in bfloat16 or wider, within the bound.
No kernel may reach another device: no remote copies, remote signals or barrier semaphores. Data moves between devices by JAX's collectives and lax.ppermute only.
A program may use at most 64 MiB of HBM per device.

```python
import jax
import jax.numpy as jnp
from jax import lax

MODEL_WIDTH = 4096
ADAPTER_RANK = 16
LAYER_COUNT = 2
S = 64
EXG = 32
EX = 512
N_GRP = 16


def touch_ends(result, key, least, high):
    longest = result.shape.index(max(result.shape))
    spots = []
    for shift in (0, 1):
        where = [jax.random.randint(jax.random.fold_in(key, axis), (), 0, length) for axis, length in enumerate(result.shape)]
        where[longest] = (where[longest] + shift) % result.shape[longest]
        spots.append(tuple(where))
    return result.at[spots[0]].set(least).at[spots[1]].set(high)


def block_levels(own_key, shape, cuts, smallest, largest):
    factor_of = 1.0
    for dim, blocks in cuts:
        draws = jax.random.uniform(jax.random.fold_in(jax.random.fold_in(own_key, 6), dim), (blocks,), jnp.float32, smallest / len(cuts), largest / len(cuts))
        factor_of = factor_of * jnp.repeat(jnp.exp(draws), shape[dim] // blocks).reshape((-1,) + (1,) * (len(shape) - 1 - dim))
    return factor_of


def scatter_about(own_key, extent, spread, limit, shards=(), held_as=jnp.bfloat16):
    gain = block_levels(own_key, extent, shards, -0.22, 0.18) if shards else 1.0
    array = jax.random.normal(own_key, extent, jnp.float32) * spread * gain
    return jnp.minimum(jnp.maximum(array, -limit), limit).astype(held_as)


def setup_inputs(seed: int = 0) -> dict:
    key_of = jax.random.split(jax.random.key(seed), 6)
    acts = scatter_about(key_of[0], (LAYER_COUNT, EX, S, MODEL_WIDTH), 1.0, 6.0, ((1, 16), (3, 32)))
    cotangents = scatter_about(key_of[1], (LAYER_COUNT, EX, S, MODEL_WIDTH), 1.0, 6.0, ((1, 16), (3, 32)))
    adapter_down_weight = scatter_about(key_of[2], (LAYER_COUNT, ADAPTER_RANK, MODEL_WIDTH), MODEL_WIDTH ** -0.5, 0.09375, ((2, 32),))
    adapter_up_weight = scatter_about(key_of[3], (LAYER_COUNT, MODEL_WIDTH, ADAPTER_RANK), MODEL_WIDTH ** -0.5, 0.09375, ((1, 32),))
    lengths = touch_ends(jax.random.randint(key_of[4], (EX,), S // 4 + 1, S + 1), jax.random.fold_in(key_of[4], 1), S // 4 + 1, S).astype(jnp.int32)
    return dict(acts=acts, cotangents=cotangents, adapter_down_weight=adapter_down_weight, adapter_up_weight=adapter_up_weight, lengths=lengths)


def block_gradients(inputs):
    xb, gb, lb, down, up = inputs
    mask = (lax.broadcasted_iota(jnp.int32, gb.shape[1:3], 1) < lb[:, None]).astype(jnp.bfloat16)
    masked_values = gb * mask[None, :, :, None]
    up_proj = jnp.einsum('mcoj,mju->mcou', masked_values.astype(jnp.float32), up.astype(jnp.float32)).astype(jnp.bfloat16)
    down_proj = jnp.einsum('bwmv,bhv->bwmh', xb.astype(jnp.float32), down.astype(jnp.float32)).astype(jnp.bfloat16)
    grad_down = jnp.einsum('lesr,lesd->elrd', up_proj.astype(jnp.float32), xb.astype(jnp.float32))
    grad_up = jnp.einsum('lesd,lesr->elrd', masked_values.astype(jnp.float32), down_proj.astype(jnp.float32))
    joined = jnp.concatenate([grad_down, grad_up], axis=2).astype(jnp.bfloat16)
    return joined.reshape(joined.shape[0], -1)

def reference(acts, cotangents, adapter_down_weight, adapter_up_weight, lengths):
    xs = acts.reshape(LAYER_COUNT, N_GRP, EXG, S, MODEL_WIDTH).transpose(1, 0, 2, 3, 4)
    gs = cotangents.reshape(LAYER_COUNT, N_GRP, EXG, S, MODEL_WIDTH).transpose(1, 0, 2, 3, 4)
    ls = lengths.reshape(N_GRP, EXG)

    def one(example_pair):
        return block_gradients((example_pair[0], example_pair[1], example_pair[2], adapter_down_weight, adapter_up_weight))
    grads = lax.map(one, (xs, gs, ls)).reshape(EX, -1)
    gram = jnp.dot(grads, grads.T, preferred_element_type=jnp.float32)
    wide = grads.astype(jnp.float32)
    sqnorm = lax.optimization_barrier(jnp.sum(wide * wide, axis=1))
    scale = lax.rsqrt(sqnorm + 1e-06)
    return gram * scale[:, None] * scale[None, :]
```

```python
import jax
import jax.numpy as jnp
from jax import lax
from jax.sharding import Mesh, PartitionSpec as P

F32 = jnp.float32
BF16 = jnp.bfloat16


def swap(block, axes):
    return lax.all_to_all(block, axes, 0, 0, tiled=True)


def local(acts, cotangents, adapter_down_weight, adapter_up_weight, lengths):
    layers, count, positions, width = acts.shape
    rank = adapter_down_weight.shape[1]
    up = jnp.einsum("lesd,ldr->lres", cotangents, adapter_up_weight, preferred_element_type=F32)
    down = jnp.einsum("lesd,lrd->lres", acts, adapter_down_weight, preferred_element_type=F32)
    live = lax.broadcasted_iota(jnp.int32, (count, positions), 1) < lengths[:, None]
    partial = jnp.where(live, jnp.stack([up, down]), 0.0)
    rows = 2 * layers * rank
    partial = partial.reshape(rows, 4, count * positions // 4).transpose(1, 0, 2)
    partial = jnp.sum(swap(partial, "y"), 0)
    partial = partial.reshape(8, rows // 8, -1)
    mine = jnp.sum(swap(partial, "zl"), 0).astype(BF16)
    whole = swap(jnp.broadcast_to(mine, (8,) + mine.shape), "zl").reshape(rows, -1)
    whole = swap(jnp.broadcast_to(whole, (4,) + whole.shape), "y")
    whole = whole.reshape(4, 2, layers, rank, count // 4, positions)
    whole = whole.transpose(1, 2, 3, 0, 4, 5).reshape(2, layers, rank, count, positions)
    grad_down = jnp.einsum("lres,lesd->lred", whole[0], acts, preferred_element_type=F32)
    grad_up = jnp.einsum("lres,lesd->lred", whole[1], cotangents, preferred_element_type=F32)
    grads = jnp.stack([grad_down, grad_up]).astype(BF16).reshape(8, rows // 8, count, width)
    own = swap(grads, ("x", "zh"))
    other = lax.ppermute(own, "c", [(0, 1), (1, 0)])
    own = own.transpose(0, 2, 1, 3).reshape(8, count, -1)
    other = other.transpose(0, 2, 1, 3).reshape(8, count, -1)
    both = jnp.stack([own, other], 1)
    gram = jnp.einsum("aek,bsfk->aebsf", own, both, preferred_element_type=F32)
    sq = jnp.sum(jnp.square(both.astype(F32)), -1)
    side = 2 * count
    gram = gram.reshape(4, side, 4, 2 * side).transpose(0, 2, 1, 3)
    row_sq = jnp.broadcast_to(sq.reshape(1, 4, 1, 2 * side), (4, 4, 1, 2 * side))
    col_sq = jnp.broadcast_to(sq[:, 0].reshape(4, 1, 1, side), (4, 4, 1, side))
    col_sq = jnp.pad(col_sq, ((0, 0), (0, 0), (0, 0), (0, side)))
    sent = jnp.concatenate([gram, row_sq, col_sq], 2).reshape(16, side + 2, 2 * side)
    got = jnp.sum(swap(sent, ("x", "y")), 0)
    ordered = got.reshape(side + 2, 2, 2, count)
    ordered = jnp.where(lax.axis_index("c") == 0, ordered, ordered[:, :, ::-1])
    half = count // 2
    tiles = ordered[:side].reshape(2, count, 8, half).transpose(0, 2, 1, 3).reshape(16, count * half)
    row_sq = jnp.broadcast_to(ordered[side].reshape(1, 8, half), (2, 8, half)).reshape(16, half)
    col_sq = jnp.broadcast_to(got[side + 1, :side].reshape(2, 1, count), (2, 8, count)).reshape(16, count)
    sent = jnp.concatenate([tiles, row_sq, col_sq], 1)
    sent = jnp.pad(sent, ((0, 0), (0, 128 - half - count))).reshape(16, -1, 128)
    got = jnp.sum(swap(sent, ("zh", "zl")), 0).reshape(-1)
    size = count * half
    tile = got[:size].reshape(count, half).T
    row_sq = got[size : size + half]
    col_sq = got[size + half : size + half + count]
    return tile * lax.rsqrt(row_sq + 1e-06)[:, None] * lax.rsqrt(col_sq + 1e-06)[None, :]


def solution(mesh):
    fine = Mesh(mesh.devices.reshape(4, 2, 2, 4, 8), ("x", "zh", "c", "y", "zl"))
    grp, hid = ("x", "zh", "c"), ("y", "zl")
    return jax.shard_map(
        local,
        mesh=fine,
        in_specs=(
            P(None, grp, None, hid),
            P(None, grp, None, hid),
            P(None, None, hid),
            P(None, hid, None),
            P(grp),
        ),
        out_specs=P(hid, grp),
        check_vma=False,
    )
```
